32 devices in a mesh: tm: 4 (over y, x), pts: 8 (over z, core).
Axes of the slice: x: 2, y: 2, z: 4, core: 2. Of those that a mesh axis runs over, the one named last changes fastest.
Arguments:
- series: bfloat16 [8192, 3, 8192], P('tm', None, 'pts'), may hold values from -6 to 6
- weights: float32 [8192], P('pts'), may hold values from 1.2207031e-05 to 0.00012207031
- freq_bins: int32 [16], replicated, may hold values from 1 to 255
Outputs:
- cross_gram: float32 [16, 2, 32, 32], P('tm')
- spatial_modes: bfloat16 [16, 2, 32, 3, 8192], P('tm', None, None, None, 'pts')
The draws below stay inside these ranges and needn't reach their ends.
All inputs are finite; a program needn't handle non-finite values.
Results may differ from the reference program's by a relative error of at most 0.0067.
Values may be sent and summed in bfloat16 or wider, within the bound.
A program may use at most 128 MiB of HBM per device.

```python
import math
import jax
import jax.numpy as jnp
from jax import lax

NFFT = 512
NB = 32
NF = 16
ITERS = 4
PT_DEV = 1024
SAMPLES = 8192
PTS = 8192


def draw_series(key, part):
    region_count = PTS // PT_DEV
    noise_key = jax.random.fold_in(key, 11)
    signal_key = jax.random.fold_in(key, 23)
    loading_key = jax.random.fold_in(key, 37)
    amp_key = jax.random.fold_in(key, 41)
    point_region = jnp.arange(PTS, dtype=jnp.int32) // PT_DEV
    region_pos = point_region.astype(jnp.float32) / max(region_count - 1, 1)
    noise = 0.7 * jax.random.normal(noise_key, (SAMPLES, 3, PTS), jnp.float32)
    signal = jax.random.normal(signal_key, (SAMPLES, region_count), jnp.float32)
    loading = jax.random.normal(loading_key, (3, region_count), jnp.float32)
    rise = 0.6 + 0.6 * region_pos
    amplitude = jax.random.uniform(amp_key, (PTS,), jnp.float32, 0.5, 1.5) * rise
    signal_points = signal[:, point_region]
    loading_points = loading[:, point_region]
    coherent = signal_points[:, None, :] * loading_points[None, :, :] * amplitude[None, None, :]
    values = jnp.clip(noise + coherent, -6.0, 6.0)
    return values.astype(jnp.bfloat16)


def plant(array, own_key, least, high):
    longest = array.shape.index(max(array.shape))
    spots = []
    for shift in (0, 1):
        where = [jax.random.randint(jax.random.fold_in(own_key, axis), (), 0, length) for axis, length in enumerate(array.shape)]
        where[longest] = (where[longest] + shift) % array.shape[longest]
        spots.append(tuple(where))
    return array.at[spots[0]].set(least).at[spots[1]].set(high)


def block_levels(stream_key, extent, shards, smallest, top_value):
    gain, own = 1.0, jax.random.fold_in(stream_key, 6)
    for position, parts in shards:
        draws = jnp.exp(jax.random.uniform(jax.random.fold_in(own, position), (parts,), jnp.float32, smallest / len(shards), top_value / len(shards)))
        gain = gain * jnp.repeat(draws, extent[position] // parts).reshape([-1 if axis == position else 1 for axis in range(len(extent))])
    return gain


def setup_inputs(seed: int = 0) -> dict:
    arg_keys = jax.random.split(jax.random.key(seed), 4)
    return {
        "series": draw_series(jax.random.fold_in(arg_keys[3], 71), 0),
        "weights": jnp.clip(jnp.exp(math.log(0.00012207031) - 2.3025851 * jax.random.uniform(arg_keys[1], (PTS,), jnp.float32) ** block_levels(arg_keys[1], (PTS,), ((0, 8),), -0.2, 0.2)), 1.220703143189894e-05, 0.00012207031),
        "freq_bins": plant(jax.random.randint(arg_keys[2], (NF,), 1, NFFT // 2), jax.random.fold_in(arg_keys[2], 1), 1, (NFFT // 2) - 1).astype(jnp.int32),
    }


def build_table(freq_bins):
    sample_index = jnp.arange(NFFT, dtype=jnp.int32)
    window = (0.5 - 0.5 * jnp.cos(2.0 * jnp.pi * sample_index.astype(jnp.float32) / NFFT)) * jnp.sqrt(8.0 / (3.0 * NFFT))
    product_index = freq_bins[:, None] * sample_index[None, :] % NFFT
    phase_angle = 2.0 * jnp.pi * product_index.astype(jnp.float32) / NFFT
    kernel_table = jnp.stack([jnp.cos(phase_angle) * window, -jnp.sin(phase_angle) * window], axis=1)
    return kernel_table.reshape(2 * NF, NFFT).astype(jnp.bfloat16)

def matmul_high(left, right):
    return jnp.matmul(left, right, precision=lax.Precision.HIGHEST)

def combine(pair_gram):
    real_part = pair_gram[..., :NB, :NB] + pair_gram[..., NB:, NB:]
    imag_part = pair_gram[..., :NB, NB:] - pair_gram[..., NB:, :NB]
    return jnp.stack([real_part, imag_part], axis=-3)

def inverse_root(cross_gram):
    real_part = cross_gram[..., 0, :, :]
    imag_part = cross_gram[..., 1, :, :]
    norm_value = jnp.sqrt(lax.optimization_barrier(jnp.sum(cross_gram * cross_gram, axis=(-3, -2, -1))))
    upper_rows = jnp.concatenate([real_part, -imag_part], axis=-1)
    lower_rows = jnp.concatenate([imag_part, real_part], axis=-1)
    current = jnp.concatenate([upper_rows, lower_rows], axis=-2) / norm_value[..., None, None]
    identity = jnp.eye(2 * NB, dtype=jnp.float32)
    inv_root = jnp.broadcast_to(identity, current.shape)
    for iteration in range(ITERS):
        factor = 0.5 * (3.0 * identity - matmul_high(inv_root, current))
        current = matmul_high(current, factor)
        inv_root = matmul_high(factor, inv_root)
    return inv_root

def reference(series, weights, freq_bins):
    kernel_table = build_table(freq_bins)
    half_len = NFFT // 2
    halves = series.reshape(NB, half_len, 3 * PTS)

    def transform(segment):
        first_half = jnp.dot(kernel_table[:, :half_len], segment, preferred_element_type=jnp.float32)
        second_half = jnp.dot(kernel_table[:, half_len:], segment, preferred_element_type=jnp.float32)
        return (first_half, second_half)
    first_half, second_half = lax.map(transform, halves)
    coefficients = (first_half + jnp.roll(second_half, -1, axis=0)).astype(jnp.bfloat16)
    stacked = jnp.transpose(coefficients.reshape(NB, NF, 2, 3 * PTS), (1, 2, 0, 3)).reshape(NF, 2 * NB, 3 * PTS)
    row_weight = jnp.tile(weights, 3)

    def solve_bin(freq_rows):
        float_rows = freq_rows.astype(jnp.float32)
        pair_gram = jnp.dot(float_rows * row_weight[None, :], float_rows.T, precision=lax.Precision.HIGHEST)
        cross_gram = combine(pair_gram)
        inv_root = inverse_root(cross_gram).astype(jnp.bfloat16)
        spatial_modes = jnp.dot(inv_root, freq_rows, preferred_element_type=jnp.float32).astype(jnp.bfloat16)
        return (cross_gram, spatial_modes)
    cross_gram, spatial_modes = lax.map(solve_bin, stacked)
    return (cross_gram, spatial_modes.reshape(NF, 2, NB, 3, PTS))
```

```python
import functools

import jax
import jax.numpy as jnp
from jax import lax
from jax.experimental import pallas as pl
from jax.experimental.pallas import tpu as pltpu
from jax.sharding import PartitionSpec as P

NFFT = 512
NB = 32
NF = 16
ITERS = 4
HALF = NFFT // 2
CHUNK = 256
MESH = pl.DeviceIdType.MESH
F32 = jnp.float32
BF16 = jnp.bfloat16


def build_table(freq_bins):
    sample_index = jnp.arange(NFFT, dtype=jnp.int32)
    window = (
        0.5 - 0.5 * jnp.cos(2.0 * jnp.pi * sample_index.astype(jnp.float32) / NFFT)
    ) * jnp.sqrt(8.0 / (3.0 * NFFT))
    product_index = freq_bins[:, None] * sample_index[None, :] % NFFT
    phase_angle = 2.0 * jnp.pi * product_index.astype(jnp.float32) / NFFT
    kernel_table = jnp.stack(
        [jnp.cos(phase_angle) * window, -jnp.sin(phase_angle) * window], axis=1
    )
    return kernel_table.reshape(2 * NF, NFFT).astype(jnp.bfloat16)


def dot_high(left, right):
    return jnp.dot(
        left, right, precision=lax.Precision.HIGHEST, preferred_element_type=F32
    )


def dot_t(left, right, **kw):
    return lax.dot_general(
        left, right, (((1,), (1,)), ((), ())), preferred_element_type=F32, **kw
    )


def eye(size):
    row = lax.broadcasted_iota(jnp.int32, (size, size), 0)
    col = lax.broadcasted_iota(jnp.int32, (size, size), 1)
    return (row == col).astype(F32)


def gather_order(rows, lb, lf):
    new = lax.broadcasted_iota(jnp.int32, (rows, rows), 0)
    old = lax.broadcasted_iota(jnp.int32, (rows, rows), 1)
    per = 2 * lf
    old_new = (old % per) * NB + old // per
    return (new == old_new).astype(F32)


def inverse_root(real, imag):
    norm = jnp.sqrt(
        jnp.sum(real * real + imag * imag, axis=(0, 1), keepdims=True)
    )
    upper = jnp.concatenate([real, -imag], axis=1)
    lower = jnp.concatenate([imag, real], axis=1)
    y = jnp.concatenate([upper, lower], axis=0) / norm
    ident = eye(2 * NB)
    z = None
    for it in range(ITERS):
        zy = y if z is None else dot_high(z, y)
        s = 0.5 * (3.0 * ident - zy)
        if it < ITERS - 1:
            y = dot_high(y, s)
        z = s if z is None else dot_high(s, z)
    return z


def kernel(nt, ns, series, table_ref, w_ref, cross_ref, modes_ref,
           xbuf, send, land, xall, grams, in_sem, a2a_send, a2a_recv,
           ar_send, ar_recv):
    t = lax.axis_index("tm")
    s = lax.axis_index("pts")
    nq = xbuf.shape[0]
    lb = NB // nt
    lf = NF // nt
    per = 2 * lf
    part = lb * per
    rows = nt * part
    for q in range(nq):
        pltpu.make_async_copy(
            series.at[:, :, pl.ds(q * CHUNK, CHUNK)], xbuf.at[q], in_sem.at[q]
        ).start()
    barrier = pltpu.get_barrier_semaphore()
    for k in range(1, nt):
        pl.semaphore_signal(barrier, inc=1, device_id={"tm": lax.rem(t + k, nt)},
                            device_id_type=MESH)
    for k in range(1, ns):
        pl.semaphore_signal(barrier, inc=1, device_id={"pts": lax.rem(s + k, ns)},
                            device_id_type=MESH)
    pl.semaphore_wait(barrier, nt + ns - 2)

    def peer_copy(q, k):
        to = lax.rem(t + k, nt)
        return pltpu.make_async_remote_copy(
            src_ref=send.at[q, to], dst_ref=land.at[q, k],
            send_sem=a2a_send.at[q, k], recv_sem=a2a_recv.at[q, k],
            device_id={"tm": to}, device_id_type=MESH,
        )

    gram = jnp.zeros((rows, rows), F32)

    def consume(q, gram):
        cols = pl.ds(q * CHUNK, CHUNK)
        for k in range(1, nt):
            peer_copy(q, k).wait_recv()
        weight = w_ref[:, q * CHUNK:(q + 1) * CHUNK]
        for c in range(3):
            for src in range(nt):
                at = lax.rem(t - src + nt, nt)
                nxt = lax.rem(t - src - 1 + nt, nt)
                main = part - 2 * per
                xall[c, src * part:src * part + main, cols] = land[q, at, c, :main, :]
                tail = land[q, at, c, main:part, :].astype(F32)
                halo = land[q, nxt, c, part:part + 2 * per, :].astype(F32)
                fixed = tail[per:] + (halo[:per] + halo[per:])
                xall[c, src * part + main:(src + 1) * part, cols] = jnp.concatenate(
                    [tail[:per], fixed], axis=0).astype(BF16)
            x = xall[c, :, cols]
            xw = x.astype(F32) * weight
            hi = xw.astype(BF16)
            lo = (xw - hi.astype(F32)).astype(BF16)
            gram = gram + dot_t(hi, x) + dot_t(lo, x)
        return gram

    for q in range(nq):
        pltpu.make_async_copy(
            series.at[:, :, pl.ds(q * CHUNK, CHUNK)], xbuf.at[q], in_sem.at[q]
        ).wait()
        for c in range(3):
            firsts, seconds = [], []
            for j in range(lb):
                block = xbuf[q, c, j * HALF:(j + 1) * HALF, :]
                both = jnp.dot(table_ref[...], block, preferred_element_type=F32)
                firsts.append(both[:2 * NF])
                seconds.append(both[2 * NF:])
            sums = [firsts[j] + seconds[j + 1] for j in range(lb - 1)]
            sums.append(firsts[lb - 1])
            halo_hi = seconds[0].astype(BF16).astype(F32)
            sums += [halo_hi, seconds[0] - halo_hi]
            for d in range(nt):
                send[q, d, c] = jnp.concatenate(
                    [v[d * per:(d + 1) * per] for v in sums], axis=0
                ).astype(BF16)
        for k in range(1, nt):
            peer_copy(q, k).start()
        land[q, 0] = send[q, t]
        if q > 0:
            gram = consume(q - 1, gram)
    gram = consume(nq - 1, gram)

    order = gather_order(rows, lb, lf)
    gram = dot_t(dot_high(order, gram), order, precision=lax.Precision.HIGHEST)
    for f in range(lf):
        a = f * 2 * NB
        b = a + NB
        e = b + NB
        grams[0, f, 0] = gram[a:b, a:b] + gram[b:e, b:e]
        grams[0, f, 1] = gram[a:b, b:e] - gram[b:e, a:b]

    def gram_copy(k):
        return pltpu.make_async_remote_copy(
            src_ref=grams.at[0], dst_ref=grams.at[k],
            send_sem=ar_send.at[k], recv_sem=ar_recv.at[k],
            device_id={"pts": lax.rem(s + k, ns)}, device_id_type=MESH,
        )

    for k in range(1, ns):
        gram_copy(k).start()
    for k in range(1, ns):
        gram_copy(k).wait_recv()
    total = grams[lax.rem(s, ns)]
    for k in range(1, ns):
        total = total + grams[lax.rem(s - k + ns, ns)]
    cross_ref[...] = total
    roots = []
    for f in range(lf):
        z = inverse_root(total[f, 0], total[f, 1]).astype(BF16).astype(F32)
        pieces = []
        if f:
            pieces.append(jnp.zeros((2 * NB, f * 2 * NB), F32))
        pieces.append(z)
        if f < lf - 1:
            pieces.append(jnp.zeros((2 * NB, (lf - 1 - f) * 2 * NB), F32))
        roots.append(jnp.concatenate(pieces, axis=1))
    mix = jnp.concatenate(roots, axis=0).astype(BF16)
    mix = jnp.dot(mix, order.astype(BF16), preferred_element_type=F32).astype(BF16)
    for c in range(3):
        for q in range(nq):
            cols = pl.ds(q * CHUNK, CHUNK)
            out = jnp.dot(mix, xall[c, :, cols], preferred_element_type=F32)
            modes_ref[:, :, c, :, cols] = out.astype(BF16).reshape(lf, 2, NB, CHUNK)
    for q in range(nq):
        for k in range(1, nt):
            peer_copy(q, k).wait_send()
    for k in range(1, ns):
        gram_copy(k).wait_send()


def on_device(nt, ns, series, weights, freq_bins):
    table = build_table(freq_bins)
    table = jnp.concatenate([table[:, :HALF], table[:, HALF:]], axis=0)
    points = series.shape[2]
    nq = points // CHUNK
    lb, lf = NB // nt, NF // nt
    rows = NB * 2 * lf
    part = lb * 2 * lf
    vmem = pl.BlockSpec(memory_space=pltpu.VMEM)
    cross, modes = pl.pallas_call(
        functools.partial(kernel, nt, ns),
        out_shape=(
            jax.ShapeDtypeStruct((lf, 2, NB, NB), F32),
            jax.ShapeDtypeStruct((lf, 2, 3, NB, points), BF16),
        ),
        in_specs=[pl.BlockSpec(memory_space=pl.ANY), vmem, vmem],
        out_specs=(vmem, vmem),
        scratch_shapes=[
            pltpu.VMEM((nq, 3, series.shape[0], CHUNK), BF16),
            pltpu.VMEM((nq, nt, 3, part + 4 * lf, CHUNK), BF16),
            pltpu.VMEM((nq, nt, 3, part + 4 * lf, CHUNK), BF16),
            pltpu.VMEM((3, rows, points), BF16),
            pltpu.VMEM((ns, lf, 2, NB, NB), F32),
            pltpu.SemaphoreType.DMA((nq,)),
            pltpu.SemaphoreType.DMA((nq, nt)),
            pltpu.SemaphoreType.DMA((nq, nt)),
            pltpu.SemaphoreType.DMA((ns,)),
            pltpu.SemaphoreType.DMA((ns,)),
        ],
        compiler_params=pltpu.CompilerParams(
            collective_id=0, has_side_effects=True, vmem_limit_bytes=56 * 2**20
        ),
    )(series.transpose(1, 0, 2), table, weights.reshape(1, points))
    return cross, modes.transpose(0, 1, 3, 2, 4)


def solution(mesh):
    nt, ns = mesh.shape["tm"], mesh.shape["pts"]
    in_specs = (P("tm", None, "pts"), P("pts"), P())
    out_specs = (P("tm", None, None, None), P("tm", None, None, None, "pts"))
    return jax.shard_map(
        functools.partial(on_device, nt, ns), mesh=mesh, in_specs=in_specs,
        out_specs=out_specs, check_vma=False
    )
```

```python
import functools

import jax
import jax.numpy as jnp
from jax import lax
from jax.experimental import pallas as pl
from jax.experimental.pallas import tpu as pltpu
from jax.sharding import PartitionSpec as P

NFFT = 512
NB = 32
NF = 16
ITERS = 4
HALF = NFFT // 2
CHUNK = 256
MESH = pl.DeviceIdType.MESH
F32 = jnp.float32
BF16 = jnp.bfloat16


def build_table(freq_bins):
    sample_index = jnp.arange(NFFT, dtype=jnp.int32)
    window = (
        0.5 - 0.5 * jnp.cos(2.0 * jnp.pi * sample_index.astype(jnp.float32) / NFFT)
    ) * jnp.sqrt(8.0 / (3.0 * NFFT))
    product_index = freq_bins[:, None] * sample_index[None, :] % NFFT
    phase_angle = 2.0 * jnp.pi * product_index.astype(jnp.float32) / NFFT
    kernel_table = jnp.stack(
        [jnp.cos(phase_angle) * window, -jnp.sin(phase_angle) * window], axis=1
    )
    return kernel_table.reshape(2 * NF, NFFT).astype(jnp.bfloat16)


def dot_high(left, right):
    return jnp.dot(
        left, right, precision=lax.Precision.HIGHEST, preferred_element_type=F32
    )


def dot_t(left, right, **kw):
    return lax.dot_general(
        left, right, (((1,), (1,)), ((), ())), preferred_element_type=F32, **kw
    )


def eye(size):
    row = lax.broadcasted_iota(jnp.int32, (size, size), 0)
    col = lax.broadcasted_iota(jnp.int32, (size, size), 1)
    return (row == col).astype(F32)


def gather_order(rows, lb, lf):
    new = lax.broadcasted_iota(jnp.int32, (rows, rows), 0)
    old = lax.broadcasted_iota(jnp.int32, (rows, rows), 1)
    per = 2 * lf
    old_new = (old % per) * NB + old // per
    return (new == old_new).astype(F32)


def inverse_root(real, imag):
    norm = jnp.sqrt(
        jnp.sum(real * real + imag * imag, axis=(0, 1), keepdims=True)
    )
    upper = jnp.concatenate([real, -imag], axis=1)
    lower = jnp.concatenate([imag, real], axis=1)
    y = jnp.concatenate([upper, lower], axis=0) / norm
    ident = eye(2 * NB)
    z = None
    for it in range(ITERS):
        zy = y if z is None else dot_high(z, y)
        s = 0.5 * (3.0 * ident - zy)
        if it < ITERS - 1:
            y = dot_high(y, s)
        z = s if z is None else dot_high(s, z)
    return z


def kernel(nt, ns, series, table_ref, w_ref, cross_ref, modes_ref,
           xbuf, send, land, xall, pair, ring, in_sem, a2a_send, a2a_recv,
           core_send, core_recv, ar_send, ar_recv):
    t = lax.axis_index("tm")
    s = lax.axis_index("pts")
    nq = xbuf.shape[0]
    lb = NB // nt
    lf = NF // nt
    per = 2 * lf
    part = lb * per
    rows = nt * part
    for q in range(nq):
        pltpu.make_async_copy(
            series.at[:, :, pl.ds(q * CHUNK, CHUNK)], xbuf.at[q], in_sem.at[q]
        ).start()
    barrier = pltpu.get_barrier_semaphore()
    for k in range(1, nt):
        pl.semaphore_signal(barrier, inc=1, device_id={"tm": lax.rem(t + k, nt)},
                            device_id_type=MESH)
    other = s + 1 - 2 * lax.rem(s, 2)
    nz = ns // 2
    pl.semaphore_signal(barrier, inc=1, device_id={"pts": other}, device_id_type=MESH)
    for k in range(1, nz):
        pl.semaphore_signal(barrier, inc=1,
                            device_id={"pts": lax.rem(s + 2 * k, ns)},
                            device_id_type=MESH)
    pl.semaphore_wait(barrier, nt - 1 + nz)

    def peer_copy(q, k):
        to = lax.rem(t + k, nt)
        return pltpu.make_async_remote_copy(
            src_ref=send.at[q, to], dst_ref=land.at[q, k],
            send_sem=a2a_send.at[q, k], recv_sem=a2a_recv.at[q, k],
            device_id={"tm": to}, device_id_type=MESH,
        )

    gram = jnp.zeros((rows, rows), F32)

    def consume(q, gram):
        cols = pl.ds(q * CHUNK, CHUNK)
        for k in range(1, nt):
            peer_copy(q, k).wait_recv()
        weight = w_ref[:, q * CHUNK:(q + 1) * CHUNK]
        halos = [
            land[q, lax.rem(t - src - 1 + nt, nt), 3 * part:, :].astype(F32)
            for src in range(nt)
        ]
        for c in range(3):
            for src in range(nt):
                at = lax.rem(t - src + nt, nt)
                main = part - 2 * per
                xall[c, src * part:src * part + main, cols] = land[q, at, c * part:c * part + main, :]
                tail = land[q, at, c * part + main:(c + 1) * part, :].astype(F32)
                fixed = tail[per:] + halos[src][c * per:(c + 1) * per]
                xall[c, src * part + main:(src + 1) * part, cols] = jnp.concatenate(
                    [tail[:per], fixed], axis=0).astype(BF16)
            x = xall[c, :, cols]
            xw = x.astype(F32) * weight
            hi = xw.astype(BF16)
            lo = (xw - hi.astype(F32)).astype(BF16)
            gram = gram + dot_t(hi, x) + dot_t(lo, x)
        return gram

    for q in range(nq):
        pltpu.make_async_copy(
            series.at[:, :, pl.ds(q * CHUNK, CHUNK)], xbuf.at[q], in_sem.at[q]
        ).wait()
        edges = []
        for c in range(3):
            firsts, seconds = [], []
            for j in range(lb):
                block = xbuf[q, c, j * HALF:(j + 1) * HALF, :]
                both = jnp.dot(table_ref[...], block, preferred_element_type=F32)
                firsts.append(both[:2 * NF])
                seconds.append(both[2 * NF:])
            sums = [firsts[j] + seconds[j + 1] for j in range(lb - 1)]
            sums.append(firsts[lb - 1])
            edges.append(seconds[0])
            for d in range(nt):
                send[q, d, c * part:(c + 1) * part, :] = jnp.concatenate(
                    [v[d * per:(d + 1) * per] for v in sums], axis=0
                ).astype(BF16)
        edges.append(jnp.zeros((2 * NF, CHUNK), F32))
        for d in range(nt):
            send[q, d, 3 * part:, :] = jnp.concatenate(
                [v[d * per:(d + 1) * per] for v in edges], axis=0
            ).astype(BF16)
        for k in range(1, nt):
            peer_copy(q, k).start()
        land[q, 0] = send[q, t]
        if q > 0:
            gram = consume(q - 1, gram)
    gram = consume(nq - 1, gram)

    order = gather_order(rows, lb, lf)
    gram = dot_t(dot_high(order, gram), order, precision=lax.Precision.HIGHEST)
    parts = []
    for f in range(lf):
        a = f * 2 * NB
        b = a + NB
        e = b + NB
        parts.append(gram[a:b, a:b] + gram[b:e, b:e])
        parts.append(gram[a:b, b:e] - gram[b:e, a:b])
    pair[0] = jnp.concatenate(parts, axis=1)

    core_copy = pltpu.make_async_remote_copy(
        src_ref=pair.at[0], dst_ref=pair.at[1], send_sem=core_send,
        recv_sem=core_recv, device_id={"pts": other}, device_id_type=MESH,
    )
    core_copy.start()
    core_copy.wait_recv()
    ring[0] = pair[0] + pair[1]

    def gram_copy(k):
        return pltpu.make_async_remote_copy(
            src_ref=ring.at[0], dst_ref=ring.at[k],
            send_sem=ar_send.at[k], recv_sem=ar_recv.at[k],
            device_id={"pts": lax.rem(s + 2 * k, ns)}, device_id_type=MESH,
        )

    for k in range(1, nz):
        gram_copy(k).start()
    for k in range(1, nz):
        gram_copy(k).wait_recv()
    chip = s // 2
    total = ring[chip]
    for k in range(1, nz):
        total = total + ring[lax.rem(chip - k + nz, nz)]
    total = [total[:, k * NB:(k + 1) * NB] for k in range(2 * lf)]
    for f in range(lf):
        cross_ref[f, 0] = total[2 * f]
        cross_ref[f, 1] = total[2 * f + 1]
    roots = []
    for f in range(lf):
        z = inverse_root(total[2 * f], total[2 * f + 1]).astype(BF16).astype(F32)
        pieces = []
        if f:
            pieces.append(jnp.zeros((2 * NB, f * 2 * NB), F32))
        pieces.append(z)
        if f < lf - 1:
            pieces.append(jnp.zeros((2 * NB, (lf - 1 - f) * 2 * NB), F32))
        roots.append(jnp.concatenate(pieces, axis=1))
    mix = jnp.concatenate(roots, axis=0).astype(BF16)
    mix = jnp.dot(mix, order.astype(BF16), preferred_element_type=F32).astype(BF16)
    for c in range(3):
        for q in range(nq):
            cols = pl.ds(q * CHUNK, CHUNK)
            out = jnp.dot(mix, xall[c, :, cols], preferred_element_type=F32)
            modes_ref[:, :, c, :, cols] = out.astype(BF16).reshape(lf, 2, NB, CHUNK)
    for q in range(nq):
        for k in range(1, nt):
            peer_copy(q, k).wait_send()
    core_copy.wait_send()
    for k in range(1, nz):
        gram_copy(k).wait_send()


def on_device(nt, ns, series, weights, freq_bins):
    table = build_table(freq_bins)
    table = jnp.concatenate([table[:, :HALF], table[:, HALF:]], axis=0)
    points = series.shape[2]
    nq = points // CHUNK
    lb, lf = NB // nt, NF // nt
    rows = NB * 2 * lf
    part = lb * 2 * lf
    vmem = pl.BlockSpec(memory_space=pltpu.VMEM)
    cross, modes = pl.pallas_call(
        functools.partial(kernel, nt, ns),
        out_shape=(
            jax.ShapeDtypeStruct((lf, 2, NB, NB), F32),
            jax.ShapeDtypeStruct((lf, 2, 3, NB, points), BF16),
        ),
        in_specs=[pl.BlockSpec(memory_space=pl.ANY), vmem, vmem],
        out_specs=(vmem, vmem),
        scratch_shapes=[
            pltpu.VMEM((nq, 3, series.shape[0], CHUNK), BF16),
            pltpu.VMEM((nq, nt, 3 * part + 8 * lf, CHUNK), BF16),
            pltpu.VMEM((nq, nt, 3 * part + 8 * lf, CHUNK), BF16),
            pltpu.VMEM((3, rows, points), BF16),
            pltpu.VMEM((2, NB, 2 * lf * NB), F32),
            pltpu.VMEM((ns // 2, NB, 2 * lf * NB), F32),
            pltpu.SemaphoreType.DMA((nq,)),
            pltpu.SemaphoreType.DMA((nq, nt)),
            pltpu.SemaphoreType.DMA((nq, nt)),
            pltpu.SemaphoreType.DMA,
            pltpu.SemaphoreType.DMA,
            pltpu.SemaphoreType.DMA((ns // 2,)),
            pltpu.SemaphoreType.DMA((ns // 2,)),
        ],
        compiler_params=pltpu.CompilerParams(
            collective_id=0, has_side_effects=True, vmem_limit_bytes=56 * 2**20
        ),
    )(series.transpose(1, 0, 2), table, weights.reshape(1, points))
    return cross, modes.transpose(0, 1, 3, 2, 4)


def solution(mesh):
    nt, ns = mesh.shape["tm"], mesh.shape["pts"]
    in_specs = (P("tm", None, "pts"), P("pts"), P())
    out_specs = (P("tm", None, None, None), P("tm", None, None, None, "pts"))
    return jax.shard_map(
        functools.partial(on_device, nt, ns), mesh=mesh, in_specs=in_specs,
        out_specs=out_specs, check_vma=False
    )
```

```python
import functools

import jax
import jax.numpy as jnp
from jax import lax
from jax.experimental import pallas as pl
from jax.experimental.pallas import tpu as pltpu
from jax.sharding import PartitionSpec as P

NFFT = 512
NB = 32
NF = 16
ITERS = 4
HALF = NFFT // 2
CHUNK = 256
MESH = pl.DeviceIdType.MESH
F32 = jnp.float32
BF16 = jnp.bfloat16


def build_table(freq_bins):
    sample_index = jnp.arange(NFFT, dtype=jnp.int32)
    window = (
        0.5 - 0.5 * jnp.cos(2.0 * jnp.pi * sample_index.astype(jnp.float32) / NFFT)
    ) * jnp.sqrt(8.0 / (3.0 * NFFT))
    product_index = freq_bins[:, None] * sample_index[None, :] % NFFT
    phase_angle = 2.0 * jnp.pi * product_index.astype(jnp.float32) / NFFT
    kernel_table = jnp.stack(
        [jnp.cos(phase_angle) * window, -jnp.sin(phase_angle) * window], axis=1
    )
    return kernel_table.reshape(2 * NF, NFFT).astype(jnp.bfloat16)


def dot_high(left, right):
    return jnp.dot(
        left, right, precision=lax.Precision.HIGHEST, preferred_element_type=F32
    )


def dot_t(left, right, **kw):
    return lax.dot_general(
        left, right, (((1,), (1,)), ((), ())), preferred_element_type=F32, **kw
    )


def eye(size):
    row = lax.broadcasted_iota(jnp.int32, (size, size), 0)
    col = lax.broadcasted_iota(jnp.int32, (size, size), 1)
    return (row == col).astype(F32)


def gather_order(rows, lb, lf):
    new = lax.broadcasted_iota(jnp.int32, (rows, rows), 0)
    old = lax.broadcasted_iota(jnp.int32, (rows, rows), 1)
    per = 2 * lf
    old_new = (old % per) * NB + old // per
    return (new == old_new).astype(F32)


def normalized(real, imag):
    norm = jnp.sqrt(
        jnp.sum(real * real + imag * imag, axis=(0, 1), keepdims=True)
    )
    upper = jnp.concatenate([real, -imag], axis=1)
    lower = jnp.concatenate([imag, real], axis=1)
    return jnp.concatenate([upper, lower], axis=0) / norm


def inverse_roots(ys):
    ident = eye(2 * NB)
    zs = None
    for it in range(ITERS):
        zys = ys if zs is None else [dot_high(z, y) for z, y in zip(zs, ys)]
        steps = [0.5 * (3.0 * ident - zy) for zy in zys]
        if it < ITERS - 1:
            ys = [dot_high(y, s) for y, s in zip(ys, steps)]
        zs = steps if zs is None else [dot_high(s, z) for s, z in zip(steps, zs)]
    return zs


def kernel(nt, ns, series, table_ref, w_ref, cross_ref, modes_ref,
           xbuf, send, land, xall, pair, ring, in_sem, a2a_send, a2a_recv,
           core_send, core_recv, ar_send, ar_recv):
    t = lax.axis_index("tm")
    s = lax.axis_index("pts")
    nq = xbuf.shape[0]
    lb = NB // nt
    lf = NF // nt
    per = 2 * lf
    part = lb * per
    rows = nt * part
    for q in range(nq):
        pltpu.make_async_copy(
            series.at[:, :, pl.ds(q * CHUNK, CHUNK)], xbuf.at[q], in_sem.at[q]
        ).start()
    barrier = pltpu.get_barrier_semaphore()
    for k in range(1, nt):
        pl.semaphore_signal(barrier, inc=1, device_id={"tm": lax.rem(t + k, nt)},
                            device_id_type=MESH)
    other = s + 1 - 2 * lax.rem(s, 2)
    nz = ns // 2
    pl.semaphore_signal(barrier, inc=1, device_id={"pts": other}, device_id_type=MESH)
    for k in range(1, nz):
        pl.semaphore_signal(barrier, inc=1,
                            device_id={"pts": lax.rem(s + 2 * k, ns)},
                            device_id_type=MESH)
    pl.semaphore_wait(barrier, nt - 1 + nz)

    def peer_copy(q, k):
        to = lax.rem(t + k, nt)
        return pltpu.make_async_remote_copy(
            src_ref=send.at[q, to], dst_ref=land.at[q, k],
            send_sem=a2a_send.at[q, k], recv_sem=a2a_recv.at[q, k],
            device_id={"tm": to}, device_id_type=MESH,
        )

    order = gather_order(rows, lb, lf).astype(BF16)
    gram = jnp.zeros((rows, rows), F32)

    def consume(q, gram):
        cols = pl.ds(q * CHUNK, CHUNK)
        for k in range(1, nt):
            peer_copy(q, k).wait_recv()
        weight = w_ref[:, q * CHUNK:(q + 1) * CHUNK]
        halos = [
            land[q, lax.rem(t - src - 1 + nt, nt), 3 * part:, :].astype(F32)
            for src in range(nt)
        ]
        for c in range(3):
            for src in range(nt):
                at = lax.rem(t - src + nt, nt)
                main = part - 2 * per
                xall[c, src * part:src * part + main, cols] = land[q, at, c * part:c * part + main, :]
                tail = land[q, at, c * part + main:(c + 1) * part, :].astype(F32)
                fixed = tail[per:] + halos[src][c * per:(c + 1) * per]
                xall[c, src * part + main:(src + 1) * part, cols] = jnp.concatenate(
                    [tail[:per], fixed], axis=0).astype(BF16)
            x = jnp.dot(
                order, xall[c, :, cols], preferred_element_type=F32
            ).astype(BF16)
            xall[c, :, cols] = x
            xw = x.astype(F32) * weight
            hi = xw.astype(BF16)
            lo = (xw - hi.astype(F32)).astype(BF16)
            gram = gram + dot_t(hi, x) + dot_t(lo, x)
        return gram

    for q in range(nq):
        pltpu.make_async_copy(
            series.at[:, :, pl.ds(q * CHUNK, CHUNK)], xbuf.at[q], in_sem.at[q]
        ).wait()
        edges = []
        for c in range(3):
            firsts, seconds = [], []
            for j in range(lb):
                block = xbuf[q, c, j * HALF:(j + 1) * HALF, :]
                both = jnp.dot(table_ref[...], block, preferred_element_type=F32)
                firsts.append(both[:2 * NF])
                seconds.append(both[2 * NF:])
            sums = [firsts[j] + seconds[j + 1] for j in range(lb - 1)]
            sums.append(firsts[lb - 1])
            edges.append(seconds[0])
            for d in range(nt):
                send[q, d, c * part:(c + 1) * part, :] = jnp.concatenate(
                    [v[d * per:(d + 1) * per] for v in sums], axis=0
                ).astype(BF16)
        edges.append(jnp.zeros((2 * NF, CHUNK), F32))
        for d in range(nt):
            send[q, d, 3 * part:, :] = jnp.concatenate(
                [v[d * per:(d + 1) * per] for v in edges], axis=0
            ).astype(BF16)
        for k in range(1, nt):
            peer_copy(q, k).start()
        land[q, 0] = send[q, t]
        if q > 0:
            gram = consume(q - 1, gram)
    gram = consume(nq - 1, gram)

    parts = []
    for f in range(lf):
        a = f * 2 * NB
        b = a + NB
        e = b + NB
        parts.append(gram[a:b, a:b] + gram[b:e, b:e])
        parts.append(gram[a:b, b:e] - gram[b:e, a:b])
    pair[0] = jnp.concatenate(parts, axis=1)

    core_copy = pltpu.make_async_remote_copy(
        src_ref=pair.at[0], dst_ref=pair.at[1], send_sem=core_send,
        recv_sem=core_recv, device_id={"pts": other}, device_id_type=MESH,
    )
    core_copy.start()
    core_copy.wait_recv()
    ring[0] = pair[0] + pair[1]

    def gram_copy(k):
        return pltpu.make_async_remote_copy(
            src_ref=ring.at[0], dst_ref=ring.at[k],
            send_sem=ar_send.at[k], recv_sem=ar_recv.at[k],
            device_id={"pts": lax.rem(s + 2 * k, ns)}, device_id_type=MESH,
        )

    for k in range(1, nz):
        gram_copy(k).start()
    for k in range(1, nz):
        gram_copy(k).wait_recv()
    chip = s // 2
    total = ring[chip]
    for k in range(1, nz):
        total = total + ring[lax.rem(chip - k + nz, nz)]
    total = [total[:, k * NB:(k + 1) * NB] for k in range(2 * lf)]
    for f in range(lf):
        cross_ref[f, 0] = total[2 * f]
        cross_ref[f, 1] = total[2 * f + 1]
    zs = inverse_roots([normalized(total[2 * f], total[2 * f + 1]) for f in range(lf)])
    roots = []
    for f in range(lf):
        z = zs[f].astype(BF16).astype(F32)
        pieces = []
        if f:
            pieces.append(jnp.zeros((2 * NB, f * 2 * NB), F32))
        pieces.append(z)
        if f < lf - 1:
            pieces.append(jnp.zeros((2 * NB, (lf - 1 - f) * 2 * NB), F32))
        roots.append(jnp.concatenate(pieces, axis=1))
    mix = jnp.concatenate(roots, axis=0).astype(BF16)
    for c in range(3):
        for q in range(nq):
            cols = pl.ds(q * CHUNK, CHUNK)
            out = jnp.dot(mix, xall[c, :, cols], preferred_element_type=F32)
            modes_ref[:, :, c, :, cols] = out.astype(BF16).reshape(lf, 2, NB, CHUNK)
    for q in range(nq):
        for k in range(1, nt):
            peer_copy(q, k).wait_send()
    core_copy.wait_send()
    for k in range(1, nz):
        gram_copy(k).wait_send()


def on_device(nt, ns, series, weights, freq_bins):
    table = build_table(freq_bins)
    table = jnp.concatenate([table[:, :HALF], table[:, HALF:]], axis=0)
    points = series.shape[2]
    nq = points // CHUNK
    lb, lf = NB // nt, NF // nt
    rows = NB * 2 * lf
    part = lb * 2 * lf
    vmem = pl.BlockSpec(memory_space=pltpu.VMEM)
    cross, modes = pl.pallas_call(
        functools.partial(kernel, nt, ns),
        out_shape=(
            jax.ShapeDtypeStruct((lf, 2, NB, NB), F32),
            jax.ShapeDtypeStruct((lf, 2, 3, NB, points), BF16),
        ),
        in_specs=[pl.BlockSpec(memory_space=pl.ANY), vmem, vmem],
        out_specs=(vmem, vmem),
        scratch_shapes=[
            pltpu.VMEM((nq, 3, series.shape[0], CHUNK), BF16),
            pltpu.VMEM((nq, nt, 3 * part + 8 * lf, CHUNK), BF16),
            pltpu.VMEM((nq, nt, 3 * part + 8 * lf, CHUNK), BF16),
            pltpu.VMEM((3, rows, points), BF16),
            pltpu.VMEM((2, NB, 2 * lf * NB), F32),
            pltpu.VMEM((ns // 2, NB, 2 * lf * NB), F32),
            pltpu.SemaphoreType.DMA((nq,)),
            pltpu.SemaphoreType.DMA((nq, nt)),
            pltpu.SemaphoreType.DMA((nq, nt)),
            pltpu.SemaphoreType.DMA,
            pltpu.SemaphoreType.DMA,
            pltpu.SemaphoreType.DMA((ns // 2,)),
            pltpu.SemaphoreType.DMA((ns // 2,)),
        ],
        compiler_params=pltpu.CompilerParams(
            collective_id=0, has_side_effects=True, vmem_limit_bytes=56 * 2**20
        ),
    )(series.transpose(1, 0, 2), table, weights.reshape(1, points))
    return cross, modes.transpose(0, 1, 3, 2, 4)


def solution(mesh):
    nt, ns = mesh.shape["tm"], mesh.shape["pts"]
    in_specs = (P("tm", None, "pts"), P("pts"), P())
    out_specs = (P("tm", None, None, None), P("tm", None, None, None, "pts"))
    return jax.shard_map(
        functools.partial(on_device, nt, ns), mesh=mesh, in_specs=in_specs,
        out_specs=out_specs, check_vma=False
    )
```

```python
import functools

import jax
import jax.numpy as jnp
from jax import lax
from jax.experimental import pallas as pl
from jax.experimental.pallas import tpu as pltpu
from jax.sharding import PartitionSpec as P

NFFT = 512
NB = 32
NF = 16
ITERS = 4
HALF = NFFT // 2
CHUNK = 256
MESH = pl.DeviceIdType.MESH
F32 = jnp.float32
BF16 = jnp.bfloat16


def build_table(freq_bins):
    sample_index = jnp.arange(NFFT, dtype=jnp.int32)
    window = (
        0.5 - 0.5 * jnp.cos(2.0 * jnp.pi * sample_index.astype(jnp.float32) / NFFT)
    ) * jnp.sqrt(8.0 / (3.0 * NFFT))
    product_index = freq_bins[:, None] * sample_index[None, :] % NFFT
    phase_angle = 2.0 * jnp.pi * product_index.astype(jnp.float32) / NFFT
    kernel_table = jnp.stack(
        [jnp.cos(phase_angle) * window, -jnp.sin(phase_angle) * window], axis=1
    )
    return kernel_table.reshape(2 * NF, NFFT).astype(jnp.bfloat16)


def dot_high(left, right):
    return jnp.dot(
        left, right, precision=lax.Precision.HIGHEST, preferred_element_type=F32
    )


def dot_t(left, right, **kw):
    return lax.dot_general(
        left, right, (((1,), (1,)), ((), ())), preferred_element_type=F32, **kw
    )


def eye(size):
    row = lax.broadcasted_iota(jnp.int32, (size, size), 0)
    col = lax.broadcasted_iota(jnp.int32, (size, size), 1)
    return (row == col).astype(F32)


def gather_order(rows, lb, lf):
    new = lax.broadcasted_iota(jnp.int32, (rows, rows), 0)
    old = lax.broadcasted_iota(jnp.int32, (rows, rows), 1)
    per = 2 * lf
    old_new = (old % per) * NB + old // per
    return (new == old_new).astype(F32)


def normalized(real, imag):
    norm = jnp.sqrt(
        jnp.sum(real * real + imag * imag, axis=(0, 1), keepdims=True)
    )
    upper = jnp.concatenate([real, -imag], axis=1)
    lower = jnp.concatenate([imag, real], axis=1)
    return jnp.concatenate([upper, lower], axis=0) / norm


def inverse_roots(ys):
    ident = eye(2 * NB)
    zs = None
    for it in range(ITERS):
        zys = ys if zs is None else [dot_high(z, y) for z, y in zip(zs, ys)]
        steps = [0.5 * (3.0 * ident - zy) for zy in zys]
        if it < ITERS - 1:
            ys = [dot_high(y, s) for y, s in zip(ys, steps)]
        zs = steps if zs is None else [dot_high(s, z) for s, z in zip(steps, zs)]
    return zs


def kernel(nt, ns, series, table_ref, w_ref, total_ref, rows_ref,
           xbuf, send, land, xall, pair, ring, in_sem, a2a_send, a2a_recv,
           core_send, core_recv, ar_send, ar_recv, row_sem):
    t = lax.axis_index("tm")
    s = lax.axis_index("pts")
    nq = xbuf.shape[0]
    lb = NB // nt
    lf = NF // nt
    per = 2 * lf
    part = lb * per
    rows = nt * part
    for q in range(nq):
        pltpu.make_async_copy(
            series.at[:, :, pl.ds(q * CHUNK, CHUNK)], xbuf.at[q], in_sem.at[q]
        ).start()
    barrier = pltpu.get_barrier_semaphore()
    for k in range(1, nt):
        pl.semaphore_signal(barrier, inc=1, device_id={"tm": lax.rem(t + k, nt)},
                            device_id_type=MESH)
    other = s + 1 - 2 * lax.rem(s, 2)
    nz = ns // 2
    pl.semaphore_signal(barrier, inc=1, device_id={"pts": other}, device_id_type=MESH)
    for k in range(1, nz):
        pl.semaphore_signal(barrier, inc=1,
                            device_id={"pts": lax.rem(s + 2 * k, ns)},
                            device_id_type=MESH)
    pl.semaphore_wait(barrier, nt - 1 + nz)

    def peer_copy(q, k):
        to = lax.rem(t + k, nt)
        return pltpu.make_async_remote_copy(
            src_ref=send.at[q, to], dst_ref=land.at[q, k],
            send_sem=a2a_send.at[q, k], recv_sem=a2a_recv.at[q, k],
            device_id={"tm": to}, device_id_type=MESH,
        )

    order = gather_order(rows, lb, lf).astype(BF16)
    gram = jnp.zeros((rows, rows), F32)

    def row_copy(q):
        cols = pl.ds(q * CHUNK, CHUNK)
        return pltpu.make_async_copy(
            xall.at[:, :, cols], rows_ref.at[:, :, cols], row_sem.at[q]
        )

    def consume(q, gram):
        cols = pl.ds(q * CHUNK, CHUNK)
        for k in range(1, nt):
            peer_copy(q, k).wait_recv()
        weight = w_ref[:, q * CHUNK:(q + 1) * CHUNK]
        halos = [
            land[q, lax.rem(t - src - 1 + nt, nt), 3 * part:, :].astype(F32)
            for src in range(nt)
        ]
        for c in range(3):
            for src in range(nt):
                at = lax.rem(t - src + nt, nt)
                main = part - 2 * per
                xall[c, src * part:src * part + main, cols] = land[q, at, c * part:c * part + main, :]
                tail = land[q, at, c * part + main:(c + 1) * part, :].astype(F32)
                fixed = tail[per:] + halos[src][c * per:(c + 1) * per]
                xall[c, src * part + main:(src + 1) * part, cols] = jnp.concatenate(
                    [tail[:per], fixed], axis=0).astype(BF16)
            x = jnp.dot(
                order, xall[c, :, cols], preferred_element_type=F32
            ).astype(BF16)
            xall[c, :, cols] = x
            xw = x.astype(F32) * weight
            hi = xw.astype(BF16)
            lo = (xw - hi.astype(F32)).astype(BF16)
            gram = gram + dot_t(hi, x) + dot_t(lo, x)
        row_copy(q).start()
        return gram

    for q in range(nq):
        pltpu.make_async_copy(
            series.at[:, :, pl.ds(q * CHUNK, CHUNK)], xbuf.at[q], in_sem.at[q]
        ).wait()
        edges = []
        for c in range(3):
            firsts, seconds = [], []
            for j in range(lb):
                block = xbuf[q, c, j * HALF:(j + 1) * HALF, :]
                both = jnp.dot(table_ref[...], block, preferred_element_type=F32)
                firsts.append(both[:2 * NF])
                seconds.append(both[2 * NF:])
            sums = [firsts[j] + seconds[j + 1] for j in range(lb - 1)]
            sums.append(firsts[lb - 1])
            edges.append(seconds[0])
            for d in range(nt):
                send[q, d, c * part:(c + 1) * part, :] = jnp.concatenate(
                    [v[d * per:(d + 1) * per] for v in sums], axis=0
                ).astype(BF16)
        edges.append(jnp.zeros((2 * NF, CHUNK), F32))
        for d in range(nt):
            send[q, d, 3 * part:, :] = jnp.concatenate(
                [v[d * per:(d + 1) * per] for v in edges], axis=0
            ).astype(BF16)
        for k in range(1, nt):
            peer_copy(q, k).start()
        land[q, 0] = send[q, t]
        if q > 0:
            gram = consume(q - 1, gram)
    gram = consume(nq - 1, gram)

    parts = []
    for f in range(lf):
        a = f * 2 * NB
        b = a + NB
        e = b + NB
        parts.append(gram[a:b, a:b] + gram[b:e, b:e])
        parts.append(gram[a:b, b:e] - gram[b:e, a:b])
    pair[0] = jnp.concatenate(parts, axis=1)

    core_copy = pltpu.make_async_remote_copy(
        src_ref=pair.at[0], dst_ref=pair.at[1], send_sem=core_send,
        recv_sem=core_recv, device_id={"pts": other}, device_id_type=MESH,
    )
    core_copy.start()
    core_copy.wait_recv()
    ring[0] = pair[0] + pair[1]

    def gram_copy(k):
        return pltpu.make_async_remote_copy(
            src_ref=ring.at[0], dst_ref=ring.at[k],
            send_sem=ar_send.at[k], recv_sem=ar_recv.at[k],
            device_id={"pts": lax.rem(s + 2 * k, ns)}, device_id_type=MESH,
        )

    for k in range(1, nz):
        gram_copy(k).start()
    for k in range(1, nz):
        gram_copy(k).wait_recv()
    chip = s // 2
    total = ring[chip]
    for k in range(1, nz):
        total = total + ring[lax.rem(chip - k + nz, nz)]
    total_ref[...] = total
    for q in range(nq):
        row_copy(q).wait()
    for q in range(nq):
        for k in range(1, nt):
            peer_copy(q, k).wait_send()
    core_copy.wait_send()
    for k in range(1, nz):
        gram_copy(k).wait_send()


def finish(total_ref, rows_ref, cross_ref, modes_ref, mix_ref):
    lf = cross_ref.shape[0]

    @pl.when(pl.program_id(0) == 0)
    def _():
        total = [total_ref[:, k * NB:(k + 1) * NB] for k in range(2 * lf)]
        for f in range(lf):
            cross_ref[f, 0] = total[2 * f]
            cross_ref[f, 1] = total[2 * f + 1]
        zs = inverse_roots(
            [normalized(total[2 * f], total[2 * f + 1]) for f in range(lf)]
        )
        roots = []
        for f in range(lf):
            z = zs[f].astype(BF16).astype(F32)
            pieces = []
            if f:
                pieces.append(jnp.zeros((2 * NB, f * 2 * NB), F32))
            pieces.append(z)
            if f < lf - 1:
                pieces.append(jnp.zeros((2 * NB, (lf - 1 - f) * 2 * NB), F32))
            roots.append(jnp.concatenate(pieces, axis=1))
        mix_ref[...] = jnp.concatenate(roots, axis=0).astype(BF16)

    for a in range(0, rows_ref.shape[2], CHUNK):
        cols = pl.ds(a, CHUNK)
        out = jnp.dot(
            mix_ref[...], rows_ref[0, :, cols], preferred_element_type=F32
        )
        modes_ref[:, :, 0, :, cols] = out.astype(BF16).reshape(lf, 2, NB, CHUNK)


def on_device(nt, ns, series, weights, freq_bins):
    table = build_table(freq_bins)
    table = jnp.concatenate([table[:, :HALF], table[:, HALF:]], axis=0)
    points = series.shape[2]
    nq = points // CHUNK
    lb, lf = NB // nt, NF // nt
    rows = NB * 2 * lf
    part = lb * 2 * lf
    vmem = pl.BlockSpec(memory_space=pltpu.VMEM)
    total, x = pl.pallas_call(
        functools.partial(kernel, nt, ns),
        out_shape=(
            jax.ShapeDtypeStruct((NB, 2 * lf * NB), F32),
            jax.ShapeDtypeStruct((3, rows, points), BF16),
        ),
        in_specs=[pl.BlockSpec(memory_space=pl.ANY), vmem, vmem],
        out_specs=(vmem, pl.BlockSpec(memory_space=pl.ANY)),
        scratch_shapes=[
            pltpu.VMEM((nq, 3, series.shape[0], CHUNK), BF16),
            pltpu.VMEM((nq, nt, 3 * part + 8 * lf, CHUNK), BF16),
            pltpu.VMEM((nq, nt, 3 * part + 8 * lf, CHUNK), BF16),
            pltpu.VMEM((3, rows, points), BF16),
            pltpu.VMEM((2, NB, 2 * lf * NB), F32),
            pltpu.VMEM((ns // 2, NB, 2 * lf * NB), F32),
            pltpu.SemaphoreType.DMA((nq,)),
            pltpu.SemaphoreType.DMA((nq, nt)),
            pltpu.SemaphoreType.DMA((nq, nt)),
            pltpu.SemaphoreType.DMA,
            pltpu.SemaphoreType.DMA,
            pltpu.SemaphoreType.DMA((ns // 2,)),
            pltpu.SemaphoreType.DMA((ns // 2,)),
            pltpu.SemaphoreType.DMA((nq,)),
        ],
        compiler_params=pltpu.CompilerParams(
            collective_id=0, has_side_effects=True, vmem_limit_bytes=56 * 2**20
        ),
    )(series.transpose(1, 0, 2), table, weights.reshape(1, points))
    cross, modes = pl.pallas_call(
        finish,
        grid=(3,),
        out_shape=(
            jax.ShapeDtypeStruct((lf, 2, NB, NB), F32),
            jax.ShapeDtypeStruct((lf, 2, 3, NB, points), BF16),
        ),
        in_specs=[
            pl.BlockSpec((NB, 2 * lf * NB), lambda c: (0, 0)),
            pl.BlockSpec((1, rows, points), lambda c: (c, 0, 0)),
        ],
        out_specs=(
            pl.BlockSpec((lf, 2, NB, NB), lambda c: (0, 0, 0, 0)),
            pl.BlockSpec((lf, 2, 1, NB, points), lambda c: (0, 0, c, 0, 0)),
        ),
        scratch_shapes=[pltpu.VMEM((rows, rows), BF16)],
        compiler_params=pltpu.CompilerParams(vmem_limit_bytes=56 * 2**20),
    )(total, x)
    return cross, modes.transpose(0, 1, 3, 2, 4)


def solution(mesh):
    nt, ns = mesh.shape["tm"], mesh.shape["pts"]
    in_specs = (P("tm", None, "pts"), P("pts"), P())
    out_specs = (P("tm", None, None, None), P("tm", None, None, None, "pts"))
    return jax.shard_map(
        functools.partial(on_device, nt, ns), mesh=mesh, in_specs=in_specs,
        out_specs=out_specs, check_vma=False
    )
```

```python
import functools

import jax
import jax.numpy as jnp
from jax import lax
from jax.experimental import pallas as pl
from jax.experimental.pallas import tpu as pltpu
from jax.sharding import PartitionSpec as P

NFFT = 512
NB = 32
NF = 16
ITERS = 4
HALF = NFFT // 2
CHUNK = 256
MESH = pl.DeviceIdType.MESH
F32 = jnp.float32
BF16 = jnp.bfloat16


def build_table(freq_bins):
    sample_index = jnp.arange(NFFT, dtype=jnp.int32)
    window = (
        0.5 - 0.5 * jnp.cos(2.0 * jnp.pi * sample_index.astype(jnp.float32) / NFFT)
    ) * jnp.sqrt(8.0 / (3.0 * NFFT))
    product_index = freq_bins[:, None] * sample_index[None, :] % NFFT
    phase_angle = 2.0 * jnp.pi * product_index.astype(jnp.float32) / NFFT
    kernel_table = jnp.stack(
        [jnp.cos(phase_angle) * window, -jnp.sin(phase_angle) * window], axis=1
    )
    return kernel_table.reshape(2 * NF, NFFT).astype(jnp.bfloat16)


def dot_high(left, right):
    return jnp.dot(
        left, right, precision=lax.Precision.HIGHEST, preferred_element_type=F32
    )


def dot_t(left, right, **kw):
    return lax.dot_general(
        left, right, (((1,), (1,)), ((), ())), preferred_element_type=F32, **kw
    )


def eye(size):
    row = lax.broadcasted_iota(jnp.int32, (size, size), 0)
    col = lax.broadcasted_iota(jnp.int32, (size, size), 1)
    return (row == col).astype(F32)


def gather_order(rows, lb, lf):
    new = lax.broadcasted_iota(jnp.int32, (rows, rows), 0)
    old = lax.broadcasted_iota(jnp.int32, (rows, rows), 1)
    per = 2 * lf
    old_new = (old % per) * NB + old // per
    return (new == old_new).astype(F32)


def normalized(real, imag):
    norm = jnp.sqrt(
        jnp.sum(real * real + imag * imag, axis=(0, 1), keepdims=True)
    )
    upper = jnp.concatenate([real, -imag], axis=1)
    lower = jnp.concatenate([imag, real], axis=1)
    return jnp.concatenate([upper, lower], axis=0) / norm


def inverse_roots(ys):
    ident = eye(2 * NB)
    zs = None
    for it in range(ITERS):
        zys = ys if zs is None else [dot_high(z, y) for z, y in zip(zs, ys)]
        steps = [0.5 * (3.0 * ident - zy) for zy in zys]
        if it < ITERS - 1:
            ys = [dot_high(y, s) for y, s in zip(ys, steps)]
        zs = steps if zs is None else [dot_high(s, z) for s, z in zip(steps, zs)]
    return zs


def kernel(nt, ns, series, table_ref, w_ref, total_ref, rows_ref,
           xbuf, send, land, xall, pair, ring, in_sem, a2a_send, a2a_recv,
           core_send, core_recv, ar_send, ar_recv, row_sem):
    t = lax.axis_index("tm")
    s = lax.axis_index("pts")
    nq = xbuf.shape[0]
    lb = NB // nt
    lf = NF // nt
    per = 2 * lf
    part = lb * per
    rows = nt * part
    peers = sorted(range(1, nt), key=lambda k: abs(2 * k - nt))

    def load(q):
        return pltpu.make_async_copy(
            series.at[:, :, pl.ds(q * CHUNK, CHUNK)], xbuf.at[q], in_sem.at[q]
        )

    load(0).start()
    barrier = pltpu.get_barrier_semaphore()
    for k in range(1, nt):
        pl.semaphore_signal(barrier, inc=1, device_id={"tm": lax.rem(t + k, nt)},
                            device_id_type=MESH)
    other = s + 1 - 2 * lax.rem(s, 2)
    nz = ns // 2
    pl.semaphore_signal(barrier, inc=1, device_id={"pts": other}, device_id_type=MESH)
    for k in range(1, nz):
        pl.semaphore_signal(barrier, inc=1,
                            device_id={"pts": lax.rem(s + 2 * k, ns)},
                            device_id_type=MESH)
    pl.semaphore_wait(barrier, nt - 1 + nz)

    def peer_copy(q, k, c):
        to = lax.rem(t + k, nt)
        sent = pl.ds(c * part, part if c < 2 else part + 4 * per)
        return pltpu.make_async_remote_copy(
            src_ref=send.at[q, to, sent], dst_ref=land.at[q, k, sent],
            send_sem=a2a_send.at[q, k, c], recv_sem=a2a_recv.at[q, k, c],
            device_id={"tm": to}, device_id_type=MESH,
        )

    order = gather_order(rows, lb, lf).astype(BF16)
    gram = jnp.zeros((rows, rows), F32)

    def row_copy(q):
        cols = pl.ds(q * CHUNK, CHUNK)
        return pltpu.make_async_copy(
            xall.at[:, :, cols], rows_ref.at[:, :, cols], row_sem.at[q]
        )

    def consume(q, gram):
        cols = pl.ds(q * CHUNK, CHUNK)
        for k in range(1, nt):
            for c in range(3):
                peer_copy(q, k, c).wait_recv()
        weight = w_ref[:, q * CHUNK:(q + 1) * CHUNK]
        halos = [
            land[q, lax.rem(t - src - 1 + nt, nt), 3 * part:, :].astype(F32)
            for src in range(nt)
        ]
        for c in range(3):
            for src in range(nt):
                at = lax.rem(t - src + nt, nt)
                main = part - 2 * per
                xall[c, src * part:src * part + main, cols] = land[q, at, c * part:c * part + main, :]
                tail = land[q, at, c * part + main:(c + 1) * part, :].astype(F32)
                fixed = tail[per:] + halos[src][c * per:(c + 1) * per]
                xall[c, src * part + main:(src + 1) * part, cols] = jnp.concatenate(
                    [tail[:per], fixed], axis=0).astype(BF16)
            x = jnp.dot(
                order, xall[c, :, cols], preferred_element_type=F32
            ).astype(BF16)
            xall[c, :, cols] = x
            xw = x.astype(F32) * weight
            hi = xw.astype(BF16)
            lo = (xw - hi.astype(F32)).astype(BF16)
            gram = gram + dot_t(hi, x) + dot_t(lo, x)
        row_copy(q).start()
        return gram

    for q in range(nq):
        load(q).wait()
        if q + 1 < nq:
            load(q + 1).start()
        edges = []
        for c in range(3):
            firsts, seconds = [], []
            for j in range(lb):
                block = xbuf[q, c, j * HALF:(j + 1) * HALF, :]
                both = jnp.dot(table_ref[...], block, preferred_element_type=F32)
                firsts.append(both[:2 * NF])
                seconds.append(both[2 * NF:])
            sums = [firsts[j] + seconds[j + 1] for j in range(lb - 1)]
            sums.append(firsts[lb - 1])
            edges.append(seconds[0])
            for d in range(nt):
                send[q, d, c * part:(c + 1) * part, :] = jnp.concatenate(
                    [v[d * per:(d + 1) * per] for v in sums], axis=0
                ).astype(BF16)
            if c == 2:
                edges.append(jnp.zeros((2 * NF, CHUNK), F32))
                for d in range(nt):
                    send[q, d, 3 * part:, :] = jnp.concatenate(
                        [v[d * per:(d + 1) * per] for v in edges], axis=0
                    ).astype(BF16)
            for k in peers:
                peer_copy(q, k, c).start()
        land[q, 0] = send[q, t]
        if q > 0:
            gram = consume(q - 1, gram)
    gram = consume(nq - 1, gram)

    parts = []
    for f in range(lf):
        a = f * 2 * NB
        b = a + NB
        e = b + NB
        parts.append(gram[a:b, a:b] + gram[b:e, b:e])
        parts.append(gram[a:b, b:e] - gram[b:e, a:b])
    pair[0] = jnp.concatenate(parts, axis=1)

    core_copy = pltpu.make_async_remote_copy(
        src_ref=pair.at[0], dst_ref=pair.at[1], send_sem=core_send,
        recv_sem=core_recv, device_id={"pts": other}, device_id_type=MESH,
    )
    core_copy.start()
    core_copy.wait_recv()
    ring[0] = pair[0] + pair[1]

    def gram_copy(k):
        return pltpu.make_async_remote_copy(
            src_ref=ring.at[0], dst_ref=ring.at[k],
            send_sem=ar_send.at[k], recv_sem=ar_recv.at[k],
            device_id={"pts": lax.rem(s + 2 * k, ns)}, device_id_type=MESH,
        )

    for k in range(1, nz):
        gram_copy(k).start()
    for k in range(1, nz):
        gram_copy(k).wait_recv()
    chip = s // 2
    total = ring[chip]
    for k in range(1, nz):
        total = total + ring[lax.rem(chip - k + nz, nz)]
    total_ref[...] = total
    for q in range(nq):
        row_copy(q).wait()
    for q in range(nq):
        for k in range(1, nt):
            for c in range(3):
                peer_copy(q, k, c).wait_send()
    core_copy.wait_send()
    for k in range(1, nz):
        gram_copy(k).wait_send()


def finish(total_ref, rows_ref, cross_ref, modes_ref, mix_ref):
    lf = cross_ref.shape[0]

    @pl.when(pl.program_id(0) == 0)
    def _():
        total = [total_ref[:, k * NB:(k + 1) * NB] for k in range(2 * lf)]
        for f in range(lf):
            cross_ref[f, 0] = total[2 * f]
            cross_ref[f, 1] = total[2 * f + 1]
        zs = inverse_roots(
            [normalized(total[2 * f], total[2 * f + 1]) for f in range(lf)]
        )
        roots = []
        for f in range(lf):
            z = zs[f].astype(BF16).astype(F32)
            pieces = []
            if f:
                pieces.append(jnp.zeros((2 * NB, f * 2 * NB), F32))
            pieces.append(z)
            if f < lf - 1:
                pieces.append(jnp.zeros((2 * NB, (lf - 1 - f) * 2 * NB), F32))
            roots.append(jnp.concatenate(pieces, axis=1))
        mix_ref[...] = jnp.concatenate(roots, axis=0).astype(BF16)

    for a in range(0, rows_ref.shape[2], CHUNK):
        cols = pl.ds(a, CHUNK)
        out = jnp.dot(
            mix_ref[...], rows_ref[0, :, cols], preferred_element_type=F32
        )
        modes_ref[:, :, 0, :, cols] = out.astype(BF16).reshape(lf, 2, NB, CHUNK)


def on_device(nt, ns, series, weights, freq_bins):
    table = build_table(freq_bins)
    table = jnp.concatenate([table[:, :HALF], table[:, HALF:]], axis=0)
    points = series.shape[2]
    nq = points // CHUNK
    lb, lf = NB // nt, NF // nt
    rows = NB * 2 * lf
    part = lb * 2 * lf
    vmem = pl.BlockSpec(memory_space=pltpu.VMEM)
    total, x = pl.pallas_call(
        functools.partial(kernel, nt, ns),
        out_shape=(
            jax.ShapeDtypeStruct((NB, 2 * lf * NB), F32),
            jax.ShapeDtypeStruct((3, rows, points), BF16),
        ),
        in_specs=[pl.BlockSpec(memory_space=pl.ANY), vmem, vmem],
        out_specs=(vmem, pl.BlockSpec(memory_space=pl.ANY)),
        scratch_shapes=[
            pltpu.VMEM((nq, 3, series.shape[0], CHUNK), BF16),
            pltpu.VMEM((nq, nt, 3 * part + 8 * lf, CHUNK), BF16),
            pltpu.VMEM((nq, nt, 3 * part + 8 * lf, CHUNK), BF16),
            pltpu.VMEM((3, rows, points), BF16),
            pltpu.VMEM((2, NB, 2 * lf * NB), F32),
            pltpu.VMEM((ns // 2, NB, 2 * lf * NB), F32),
            pltpu.SemaphoreType.DMA((nq,)),
            pltpu.SemaphoreType.DMA((nq, nt, 3)),
            pltpu.SemaphoreType.DMA((nq, nt, 3)),
            pltpu.SemaphoreType.DMA,
            pltpu.SemaphoreType.DMA,
            pltpu.SemaphoreType.DMA((ns // 2,)),
            pltpu.SemaphoreType.DMA((ns // 2,)),
            pltpu.SemaphoreType.DMA((nq,)),
        ],
        compiler_params=pltpu.CompilerParams(
            collective_id=0, has_side_effects=True, vmem_limit_bytes=56 * 2**20
        ),
    )(series.transpose(1, 0, 2), table, weights.reshape(1, points))
    cross, modes = pl.pallas_call(
        finish,
        grid=(3,),
        out_shape=(
            jax.ShapeDtypeStruct((lf, 2, NB, NB), F32),
            jax.ShapeDtypeStruct((lf, 2, 3, NB, points), BF16),
        ),
        in_specs=[
            pl.BlockSpec((NB, 2 * lf * NB), lambda c: (0, 0)),
            pl.BlockSpec((1, rows, points), lambda c: (c, 0, 0)),
        ],
        out_specs=(
            pl.BlockSpec((lf, 2, NB, NB), lambda c: (0, 0, 0, 0)),
            pl.BlockSpec((lf, 2, 1, NB, points), lambda c: (0, 0, c, 0, 0)),
        ),
        scratch_shapes=[pltpu.VMEM((rows, rows), BF16)],
        compiler_params=pltpu.CompilerParams(vmem_limit_bytes=56 * 2**20),
    )(total, x)
    return cross, modes.transpose(0, 1, 3, 2, 4)


def solution(mesh):
    nt, ns = mesh.shape["tm"], mesh.shape["pts"]
    in_specs = (P("tm", None, "pts"), P("pts"), P())
    out_specs = (P("tm", None, None, None), P("tm", None, None, None, "pts"))
    return jax.shard_map(
        functools.partial(on_device, nt, ns), mesh=mesh, in_specs=in_specs,
        out_specs=out_specs, check_vma=False
    )
```

```python
import functools

import jax
import jax.numpy as jnp
from jax import lax
from jax.experimental import pallas as pl
from jax.experimental.pallas import tpu as pltpu
from jax.sharding import PartitionSpec as P

NFFT = 512
NB = 32
NF = 16
ITERS = 4
HALF = NFFT // 2
CHUNK = 256
MESH = pl.DeviceIdType.MESH
F32 = jnp.float32
BF16 = jnp.bfloat16


def build_table(freq_bins):
    sample_index = jnp.arange(NFFT, dtype=jnp.int32)
    window = (
        0.5 - 0.5 * jnp.cos(2.0 * jnp.pi * sample_index.astype(jnp.float32) / NFFT)
    ) * jnp.sqrt(8.0 / (3.0 * NFFT))
    product_index = freq_bins[:, None] * sample_index[None, :] % NFFT
    phase_angle = 2.0 * jnp.pi * product_index.astype(jnp.float32) / NFFT
    kernel_table = jnp.stack(
        [jnp.cos(phase_angle) * window, -jnp.sin(phase_angle) * window], axis=1
    )
    return kernel_table.reshape(2 * NF, NFFT).astype(jnp.bfloat16)


def dot_high(left, right):
    return jnp.dot(
        left, right, precision=lax.Precision.HIGHEST, preferred_element_type=F32
    )


def dot_t(left, right, **kw):
    return lax.dot_general(
        left, right, (((1,), (1,)), ((), ())), preferred_element_type=F32, **kw
    )


def eye(size):
    row = lax.broadcasted_iota(jnp.int32, (size, size), 0)
    col = lax.broadcasted_iota(jnp.int32, (size, size), 1)
    return (row == col).astype(F32)


def gather_order(rows, lb, lf):
    new = lax.broadcasted_iota(jnp.int32, (rows, rows), 0)
    old = lax.broadcasted_iota(jnp.int32, (rows, rows), 1)
    per = 2 * lf
    old_new = (old % per) * NB + old // per
    return (new == old_new).astype(F32)


def normalized(real, imag):
    norm = jnp.sqrt(
        jnp.sum(real * real + imag * imag, axis=(0, 1), keepdims=True)
    )
    upper = jnp.concatenate([real, -imag], axis=1)
    lower = jnp.concatenate([imag, real], axis=1)
    return jnp.concatenate([upper, lower], axis=0) / norm


def inverse_roots(ys):
    ident = eye(2 * NB)
    zs = None
    for it in range(ITERS):
        zys = ys if zs is None else [dot_high(z, y) for z, y in zip(zs, ys)]
        steps = [0.5 * (3.0 * ident - zy) for zy in zys]
        if it < ITERS - 1:
            ys = [dot_high(y, s) for y, s in zip(ys, steps)]
        zs = steps if zs is None else [dot_high(s, z) for s, z in zip(steps, zs)]
    return zs


def kernel(nt, ns, series, table_ref, w_ref, total_ref, rows_ref,
           xbuf, send, land, xall, pair, ring, in_sem, a2a_send, a2a_recv,
           core_send, core_recv, ar_send, ar_recv, row_sem):
    t = lax.axis_index("tm")
    s = lax.axis_index("pts")
    points = xbuf.shape[2]
    cuts = [0, *range(CHUNK // 2, points, CHUNK), points]
    nq = len(cuts) - 1

    def span(q):
        return pl.ds(cuts[q], cuts[q + 1] - cuts[q])

    lb = NB // nt
    lf = NF // nt
    per = 2 * lf
    part = lb * per
    rows = nt * part
    for q in range(nq):
        pltpu.make_async_copy(
            series.at[:, :, span(q)], xbuf.at[:, :, span(q)], in_sem.at[q]
        ).start()
    barrier = pltpu.get_barrier_semaphore()
    for k in range(1, nt):
        pl.semaphore_signal(barrier, inc=1, device_id={"tm": lax.rem(t + k, nt)},
                            device_id_type=MESH)
    other = s + 1 - 2 * lax.rem(s, 2)
    nz = ns // 2
    pl.semaphore_signal(barrier, inc=1, device_id={"pts": other}, device_id_type=MESH)
    for k in range(1, nz):
        pl.semaphore_signal(barrier, inc=1,
                            device_id={"pts": lax.rem(s + 2 * k, ns)},
                            device_id_type=MESH)
    pl.semaphore_wait(barrier, nt - 1 + nz)

    def peer_copy(q, k):
        to = lax.rem(t + k, nt)
        return pltpu.make_async_remote_copy(
            src_ref=send.at[to, :, span(q)], dst_ref=land.at[k, :, span(q)],
            send_sem=a2a_send.at[q, k], recv_sem=a2a_recv.at[q, k],
            device_id={"tm": to}, device_id_type=MESH,
        )

    order = gather_order(rows, lb, lf).astype(BF16)
    gram = jnp.zeros((rows, rows), F32)

    def row_copy(q):
        cols = span(q)
        return pltpu.make_async_copy(
            xall.at[:, :, cols], rows_ref.at[:, :, cols], row_sem.at[q]
        )

    def consume(q, gram):
        cols = span(q)
        for k in range(1, nt):
            peer_copy(q, k).wait_recv()
        weight = w_ref[:, cols]
        halos = [
            land[lax.rem(t - src - 1 + nt, nt), 3 * part:, cols].astype(F32)
            for src in range(nt)
        ]
        for c in range(3):
            for src in range(nt):
                at = lax.rem(t - src + nt, nt)
                main = part - 2 * per
                xall[c, src * part:src * part + main, cols] = land[at, c * part:c * part + main, cols]
                tail = land[at, c * part + main:(c + 1) * part, cols].astype(F32)
                fixed = tail[per:] + halos[src][c * per:(c + 1) * per]
                xall[c, src * part + main:(src + 1) * part, cols] = jnp.concatenate(
                    [tail[:per], fixed], axis=0).astype(BF16)
            x = jnp.dot(
                order, xall[c, :, cols], preferred_element_type=F32
            ).astype(BF16)
            xall[c, :, cols] = x
            xw = x.astype(F32) * weight
            hi = xw.astype(BF16)
            lo = (xw - hi.astype(F32)).astype(BF16)
            gram = gram + dot_t(hi, x) + dot_t(lo, x)
        row_copy(q).start()
        return gram

    for q in range(nq):
        pltpu.make_async_copy(
            series.at[:, :, span(q)], xbuf.at[:, :, span(q)], in_sem.at[q]
        ).wait()
        edges = []
        for c in range(3):
            firsts, seconds = [], []
            for j in range(lb):
                block = xbuf[c, j * HALF:(j + 1) * HALF, span(q)]
                both = jnp.dot(table_ref[...], block, preferred_element_type=F32)
                firsts.append(both[:2 * NF])
                seconds.append(both[2 * NF:])
            sums = [firsts[j] + seconds[j + 1] for j in range(lb - 1)]
            sums.append(firsts[lb - 1])
            edges.append(seconds[0])
            for d in range(nt):
                send[d, c * part:(c + 1) * part, span(q)] = jnp.concatenate(
                    [v[d * per:(d + 1) * per] for v in sums], axis=0
                ).astype(BF16)
        edges.append(jnp.zeros(edges[0].shape, F32))
        for d in range(nt):
            send[d, 3 * part:, span(q)] = jnp.concatenate(
                [v[d * per:(d + 1) * per] for v in edges], axis=0
            ).astype(BF16)
        for k in range(1, nt):
            peer_copy(q, k).start()
        land[0, :, span(q)] = send[t, :, span(q)]
        if q > 0:
            gram = consume(q - 1, gram)
    gram = consume(nq - 1, gram)

    parts = []
    for f in range(lf):
        a = f * 2 * NB
        b = a + NB
        e = b + NB
        parts.append(gram[a:b, a:b] + gram[b:e, b:e])
        parts.append(gram[a:b, b:e] - gram[b:e, a:b])
    pair[0] = jnp.concatenate(parts, axis=1)

    core_copy = pltpu.make_async_remote_copy(
        src_ref=pair.at[0], dst_ref=pair.at[1], send_sem=core_send,
        recv_sem=core_recv, device_id={"pts": other}, device_id_type=MESH,
    )
    core_copy.start()
    core_copy.wait_recv()
    ring[0] = pair[0] + pair[1]

    def gram_copy(k):
        return pltpu.make_async_remote_copy(
            src_ref=ring.at[0], dst_ref=ring.at[k],
            send_sem=ar_send.at[k], recv_sem=ar_recv.at[k],
            device_id={"pts": lax.rem(s + 2 * k, ns)}, device_id_type=MESH,
        )

    for k in range(1, nz):
        gram_copy(k).start()
    for k in range(1, nz):
        gram_copy(k).wait_recv()
    chip = s // 2
    total = ring[chip]
    for k in range(1, nz):
        total = total + ring[lax.rem(chip - k + nz, nz)]
    total_ref[...] = total
    for q in range(nq):
        row_copy(q).wait()
    for q in range(nq):
        for k in range(1, nt):
            peer_copy(q, k).wait_send()
    core_copy.wait_send()
    for k in range(1, nz):
        gram_copy(k).wait_send()


def finish(total_ref, rows_ref, cross_ref, modes_ref, mix_ref):
    lf = cross_ref.shape[0]

    @pl.when(pl.program_id(0) == 0)
    def _():
        total = [total_ref[:, k * NB:(k + 1) * NB] for k in range(2 * lf)]
        for f in range(lf):
            cross_ref[f, 0] = total[2 * f]
            cross_ref[f, 1] = total[2 * f + 1]
        zs = inverse_roots(
            [normalized(total[2 * f], total[2 * f + 1]) for f in range(lf)]
        )
        roots = []
        for f in range(lf):
            z = zs[f].astype(BF16).astype(F32)
            pieces = []
            if f:
                pieces.append(jnp.zeros((2 * NB, f * 2 * NB), F32))
            pieces.append(z)
            if f < lf - 1:
                pieces.append(jnp.zeros((2 * NB, (lf - 1 - f) * 2 * NB), F32))
            roots.append(jnp.concatenate(pieces, axis=1))
        mix_ref[...] = jnp.concatenate(roots, axis=0).astype(BF16)

    for a in range(0, rows_ref.shape[2], CHUNK):
        cols = pl.ds(a, CHUNK)
        out = jnp.dot(
            mix_ref[...], rows_ref[0, :, cols], preferred_element_type=F32
        )
        modes_ref[:, :, 0, :, cols] = out.astype(BF16).reshape(lf, 2, NB, CHUNK)


def on_device(nt, ns, series, weights, freq_bins):
    table = build_table(freq_bins)
    table = jnp.concatenate([table[:, :HALF], table[:, HALF:]], axis=0)
    points = series.shape[2]
    nq = points // CHUNK + 1
    lb, lf = NB // nt, NF // nt
    rows = NB * 2 * lf
    part = lb * 2 * lf
    vmem = pl.BlockSpec(memory_space=pltpu.VMEM)
    total, x = pl.pallas_call(
        functools.partial(kernel, nt, ns),
        out_shape=(
            jax.ShapeDtypeStruct((NB, 2 * lf * NB), F32),
            jax.ShapeDtypeStruct((3, rows, points), BF16),
        ),
        in_specs=[pl.BlockSpec(memory_space=pl.ANY), vmem, vmem],
        out_specs=(vmem, pl.BlockSpec(memory_space=pl.ANY)),
        scratch_shapes=[
            pltpu.VMEM((3, series.shape[0], points), BF16),
            pltpu.VMEM((nt, 3 * part + 8 * lf, points), BF16),
            pltpu.VMEM((nt, 3 * part + 8 * lf, points), BF16),
            pltpu.VMEM((3, rows, points), BF16),
            pltpu.VMEM((2, NB, 2 * lf * NB), F32),
            pltpu.VMEM((ns // 2, NB, 2 * lf * NB), F32),
            pltpu.SemaphoreType.DMA((nq,)),
            pltpu.SemaphoreType.DMA((nq, nt)),
            pltpu.SemaphoreType.DMA((nq, nt)),
            pltpu.SemaphoreType.DMA,
            pltpu.SemaphoreType.DMA,
            pltpu.SemaphoreType.DMA((ns // 2,)),
            pltpu.SemaphoreType.DMA((ns // 2,)),
            pltpu.SemaphoreType.DMA((nq,)),
        ],
        compiler_params=pltpu.CompilerParams(
            collective_id=0, has_side_effects=True, vmem_limit_bytes=56 * 2**20
        ),
    )(series.transpose(1, 0, 2), table, weights.reshape(1, points))
    cross, modes = pl.pallas_call(
        finish,
        grid=(3,),
        out_shape=(
            jax.ShapeDtypeStruct((lf, 2, NB, NB), F32),
            jax.ShapeDtypeStruct((lf, 2, 3, NB, points), BF16),
        ),
        in_specs=[
            pl.BlockSpec((NB, 2 * lf * NB), lambda c: (0, 0)),
            pl.BlockSpec((1, rows, points), lambda c: (c, 0, 0)),
        ],
        out_specs=(
            pl.BlockSpec((lf, 2, NB, NB), lambda c: (0, 0, 0, 0)),
            pl.BlockSpec((lf, 2, 1, NB, points), lambda c: (0, 0, c, 0, 0)),
        ),
        scratch_shapes=[pltpu.VMEM((rows, rows), BF16)],
        compiler_params=pltpu.CompilerParams(vmem_limit_bytes=56 * 2**20),
    )(total, x)
    return cross, modes.transpose(0, 1, 3, 2, 4)


def solution(mesh):
    nt, ns = mesh.shape["tm"], mesh.shape["pts"]
    in_specs = (P("tm", None, "pts"), P("pts"), P())
    out_specs = (P("tm", None, None, None), P("tm", None, None, None, "pts"))
    return jax.shard_map(
        functools.partial(on_device, nt, ns), mesh=mesh, in_specs=in_specs,
        out_specs=out_specs, check_vma=False
    )
```
